512 devices in a mesh: lon: 32 (over z, y_lo), lat: 16 (over x, y_hi, core).
Axes of the slice: x: 4, y: 8 (y_hi: 2, y_lo: 4; y = y_hi * 4 + y_lo), z: 8, core: 2. Of those that a mesh axis runs over, the one named last changes fastest.
Arguments:
- cotangent: float32 [4, 2048, 4096], P(None, 'lat', 'lon'), may hold values from -6 to 6
- coefficients: bfloat16 [9, 4, 2048, 4096], P(None, None, 'lat', 'lon'), may hold values from -2 to 2
- wet_mask: int32 [4, 2048, 4096], P(None, 'lat', 'lon'), may hold values 0 or 1
Outputs:
- gradient: float32 [4, 2048, 4096], P(None, 'lat', 'lon')
The draws below stay inside these ranges and needn't reach their ends.
All inputs are finite; a program needn't handle non-finite values. No bound on the sum of `wet_mask` on one device may be relied on, other than what follows from the above.
Results may differ from the reference program's by a relative error of at most 0.0003.
Values sent between devices are 32-bit elements; how exact they have to be, the bound alone decides.
No kernel may reach another device: no remote copies, remote signals or barrier semaphores. Data moves between devices by JAX's collectives and lax.ppermute only.
A program may use at most 64 MiB of HBM per device.

```python
import jax
import jax.numpy as jnp
from jax import lax

LEV = 4
ITERS = 8
NY = 2048
NX = 4096


def draw_coefficients(key, part):
    key = jax.random.fold_in(key, 7)
    centre_key, around_key = jax.random.split(key)
    centre = 1.0 + jax.random.uniform(centre_key, (1, LEV, NY, NX), jnp.float32, -0.3, 0.3)
    beside_all = 0.2 * jnp.clip(jax.random.normal(around_key, (8, LEV, NY, NX), jnp.float32), -3.0, 3.0)
    return jnp.concatenate([beside_all[:4], centre, beside_all[4:]], axis=0).astype(jnp.bfloat16)


def place_ends(result, stream_key, smallest, largest):
    longest = result.shape.index(max(result.shape))
    spots = []
    for shift in (0, 1):
        where = [jax.random.randint(jax.random.fold_in(stream_key, axis), (), 0, length) for axis, length in enumerate(result.shape)]
        where[longest] = (where[longest] + shift) % result.shape[longest]
        spots.append(tuple(where))
    return result.at[spots[0]].set(smallest).at[spots[1]].set(largest)


def block_scale(own_key, shape, pieces, least, top_value):
    factor_of, own = 1.0, jax.random.fold_in(own_key, 6)
    for dim, parts in pieces:
        heights = jnp.exp(jax.random.uniform(jax.random.fold_in(own, dim), (parts,), jnp.float32, least / len(pieces), top_value / len(pieces)))
        factor_of = factor_of * jnp.repeat(heights, shape[dim] // parts).reshape([-1 if axis == dim else 1 for axis in range(len(shape))])
    return factor_of


def gaussian(rng, extent, scale, reach, cuts=(), held_as=jnp.bfloat16):
    values = scale * jax.random.normal(rng, extent, jnp.float32)
    if cuts:
        values = values * block_scale(rng, extent, cuts, -0.22, 0.18)
    return jnp.clip(values, -reach, reach).astype(held_as)


def setup_inputs(seed: int = 0) -> dict:
    keys = jax.random.split(jax.random.key(seed), 4)
    cotangent = gaussian(keys[0], (LEV, NY, NX), 1.0, 6.0, ((1, 16), (2, 32)), jnp.float32)
    coefficients = draw_coefficients(jax.random.fold_in(keys[3], 71), 0)
    wet_mask = place_ends((jax.random.randint(keys[2], (LEV, NY, NX), 0, 4) < 3).astype(jnp.int32), jax.random.fold_in(keys[2], 1), 0, 1)
    return {"cotangent": cotangent, "coefficients": coefficients, "wet_mask": wet_mask}


OFFSETS = [(-1, -1), (-1, 0), (-1, 1), (0, -1), (0, 0), (0, 1), (1, -1), (1, 0), (1, 1)]


def extend(field):
    top_rim = field[..., -1:, ::-1]
    bottom_rim = jnp.zeros_like(field[..., :1, :])
    rows_done = jnp.concatenate([bottom_rim, field, top_rim], axis=-2)
    return jnp.concatenate([rows_done[..., -1:], rows_done, rows_done[..., :1]], axis=-1)


def adjoint_step(field, weights, wet):
    num_rows, num_cols = field.shape
    products = weights * (wet * field)[None]
    extended = extend(products)
    total = jnp.zeros_like(field)
    for offset, (row_step, col_step) in enumerate(OFFSETS):
        total = total + extended[offset, 1 - row_step:1 - row_step + num_rows, 1 - col_step:1 - col_step + num_cols]
    return wet * total


def reference(cotangent, coefficients, wet_mask):
    def one_level(level):
        weights = lax.dynamic_index_in_dim(coefficients, level, 1, keepdims=False).astype(jnp.float32)
        wet = lax.dynamic_index_in_dim(wet_mask, level, 0, keepdims=False).astype(jnp.float32)
        field = lax.dynamic_index_in_dim(cotangent, level, 0, keepdims=False)
        for iteration in range(ITERS):
            field = adjoint_step(field, weights, wet)
        return field

    return lax.map(one_level, jnp.arange(LEV, dtype=jnp.int32))
```

```python
import jax
import jax.numpy as jnp
from jax import lax
from jax.experimental import pallas as pl
from jax.experimental.pallas import tpu as pltpu
from jax.sharding import PartitionSpec as P


STEPS = 8
LEVELS = 4
SIZE = 128
TILES = LEVELS + 1
F32 = jnp.float32


def dc_of(c):
    return c % 3 - 1


def lanes(rows):
    return lax.broadcasted_iota(jnp.int32, (rows, SIZE), 1)


def sublanes(rows):
    return lax.broadcasted_iota(jnp.int32, (rows, SIZE), 0)


def turn(x, shift, axis=1):
    shift = shift % x.shape[axis]
    return x if shift == 0 else pltpu.roll(x, shift, axis)


def seam(level, dc):
    return 16 * level + (8 if dc == 1 else 7)


def join(mains, rim, dc, lane):
    if dc == 0:
        return list(mains) + [rim]
    fixed, new_rim = [], rim
    for level in range(LEVELS):
        here = lane == seam(level, dc)
        fixed.append(jnp.where(here, rim, mains[level]))
        new_rim = jnp.where(here, mains[level], new_rim)
    return fixed + [new_rim]


def shifted(tiles, dc, lane):
    return join([turn(t, dc) for t in tiles[:LEVELS]], turn(tiles[LEVELS], dc), dc, lane)


def source(v, level, block, cot, coef, wet, is_top):
    rows = slice(16 * block, 16 * block + 16)
    if v == 9:
        return cot[level, rows, :]
    x = coef[v, level, rows, :].astype(F32)
    if block == SIZE // 16 - 1 and v >= 6:
        other = coef[8 - v, level, rows, :].astype(F32)
        x = jnp.where((sublanes(16) == 15) & is_top, other, x)
    return x * wet[level, rows, :].astype(F32)


def pack_lon(cot, coef, wet, pay1, pay2):
    is_top = lax.axis_index("lat") == lax.axis_size("lat") - 1
    even = lax.axis_index("lon") % 2 == 0
    lane = lanes(16)
    first = (lane & 8) == 0

    def both_edges(pair, block):
        out = None
        for half in (0, 1):
            for level in range(LEVELS):
                x = source(2 * pair + half, level, block, cot, coef, wet, is_top)
                x = turn(x, 64 * half + 16 * level + 8)
                out = x if out is None else jnp.where((lane >> 4) == 4 * half + level, x, out)
        return out

    def put(row, a, b):
        east = jnp.where(first, a, turn(b, 8))
        west = jnp.where(first, turn(b, -8), a)
        pay1[row : row + 16, :] = jnp.where(even, east, west)
        pay2[row : row + 16, :] = jnp.where(even, west, east)

    for block in range(8):
        put(16 * block, both_edges(0, block), both_edges(1, block))
        put(128 + 16 * block, both_edges(2, block), both_edges(3, block))
    for block in range(4):
        put(256 + 16 * block, both_edges(4, block), both_edges(4, block + 4))


def rotate_main(cot, coef, wet, token, out):
    del token
    is_top = lax.axis_index("lat") == lax.axis_size("lat") - 1
    for block in range(8):
        rows = slice(16 * block, 16 * block + 16)
        for v in range(10):
            for level in range(LEVELS):
                x = source(v, level, block, cot, coef, wet, is_top)
                if v < 9:
                    out[v, level, rows, :] = turn(x, 16 * level + 8 + dc_of(v))
                else:
                    for dc in (-1, 0, 1):
                        out[10 + dc, level, rows, :] = turn(x, 16 * level + 8 + dc)


def rims(got1, got2, even, block, lane):
    first = (lane & 8) == 0
    res = []
    for pair in range(5):
        if pair < 4:
            row, second = 128 * (pair // 2) + 16 * block, pair % 2 == 1
        else:
            row, second = 256 + 16 * (block % 4), block >= 4
        one, two = got1[row : row + 16, :], got2[row : row + 16, :]
        from_east = jnp.where(even, one, two)
        from_west = jnp.where(even, two, one)
        if second:
            from_west, from_east = turn(from_west, -8), turn(from_east, 8)
        res.append(jnp.where(first, from_west, from_east))
    return res


def tiles_of(main, rim_tiles, block, lane, which):
    rows = slice(16 * block, 16 * block + 16)
    res = []
    for v, dc in which:
        at = v if v < 9 else 10 + dc
        rim = turn(rim_tiles[v // 2], dc + 64 * (v % 2))
        res.append(join([main[at, level, rows, :] for level in range(LEVELS)], rim, dc, lane))
    return res


COEFS = [(c, dc_of(c)) for c in range(9)]


def pack_lat(main, got1, got2, pay1, pay2):
    lat = lax.axis_index("lat")
    even_lon = lax.axis_index("lon") % 2 == 0
    even = lat % 2 == 0
    is_top = lat == lax.axis_size("lat") - 1
    lane = lanes(16)
    which = COEFS + [(9, 0)]
    low = tiles_of(main, rims(got1, got2, even_lon, 0, lane), 0, lane, which)
    high = tiles_of(main, rims(got1, got2, even_lon, 7, lane), 7, lane, which)
    for v in range(10):
        for tile in range(TILES):
            south, north = low[v][tile][:8], high[v][tile][8:]
            pay1[v, tile] = jnp.where(even, north, south)
            pay2[v, tile] = jnp.where(even, south, north)

    @pl.when(is_top)
    def _():
        lane8, row8 = lanes(8), sublanes(8)
        for v in range(10):
            for tile in range(TILES):
                x = high[v][tile][8:]
                index = (lane8 ^ 15) if tile == LEVELS else ((143 + 32 * tile - lane8) & 127)
                x = jnp.take_along_axis(x, index, axis=1, mode="promise_in_bounds")
                x = jnp.take_along_axis(x, 7 - row8, axis=0, mode="promise_in_bounds")
                pay2[8 - v if v < 9 else 9, tile] = x


def sums(coef_tiles, field_tiles):
    res = []
    for dr in range(3):
        total = coef_tiles(3 * dr) * field_tiles[0]
        for dc in (1, 2):
            total = total + coef_tiles(3 * dr + dc) * field_tiles[dc]
        res.append(total)
    return res


def north_of(before, here, row):
    x = turn(here, 1, 0)
    return x if before is None else jnp.where(row == 0, turn(before, 1, 0), x)


def south_of(here, after, row):
    x = turn(here, -1, 0)
    return x if after is None else jnp.where(row == 7, turn(after, -1, 0), x)


def inner(main, got1, got2, wet, token, edge_coef, edge_field, saved, result, edge_wet, coef, field):
    del token
    even_lon = lax.axis_index("lon") % 2 == 0
    lane16 = lanes(16)
    for block in range(8):
        rows = slice(16 * block, 16 * block + 16)
        rim_tiles = rims(got1, got2, even_lon, block, lane16)
        built = tiles_of(main, rim_tiles, block, lane16, COEFS + [(9, -1), (9, 0), (9, 1)])
        for v in range(12):
            for tile in range(TILES):
                x = built[v][tile]
                if v < 9:
                    coef[v, tile, rows, :] = x
                else:
                    field[v - 9, tile, rows, :] = x
                if block in (0, 7):
                    side, part = (0, x[:8]) if block == 0 else (1, x[8:])
                    if v < 9:
                        edge_coef[v, side, tile] = part
                    else:
                        edge_field[v - 9, side, tile] = part
    for level in range(LEVELS):
        edge_wet[0, level] = wet[level, :8, :].astype(F32)
        edge_wet[1, level] = wet[level, SIZE - 8 :, :].astype(F32)

    lane, row = lanes(8), sublanes(8)

    def step(k, last):
        done = [None] * TILES
        older = [[None] * TILES, [None] * TILES]
        for t in range(17):
            now = []
            for tile in range(TILES):
                if t < 16:
                    rows = slice(8 * t, 8 * t + 8)
                    now.append(sums(lambda c: coef[c, tile, rows, :], [field[dc, tile, rows, :] for dc in range(3)]))
            if t < 16:
                for tile in range(TILES):
                    if t == 1:
                        saved[k, 0, tile] = now[tile][0]
                    if t == 14:
                        saved[k, 1, tile] = now[tile][2]
            if t >= 1 and not (last and t - 1 in (0, 15)):
                new = []
                for tile in range(TILES):
                    after = now[tile][0] if t < 16 else None
                    new.append(done[tile] + south_of(older[0][tile], after, row))
                rows = slice(8 * (t - 1), 8 * t)
                if last:
                    for level in range(LEVELS):
                        mask = wet[level, rows, :].astype(F32)
                        result[level, rows, :] = mask * turn(new[level], -(16 * level + 8))
                else:
                    for dc in (-1, 0, 1):
                        for tile, x in enumerate(new if dc == 0 else shifted(new, dc, lane)):
                            field[dc + 1, tile, rows, :] = x
            if t < 16:
                for tile in range(TILES):
                    done[tile] = now[tile][1] + north_of(older[1][tile], now[tile][2], row)
                    older[0][tile], older[1][tile] = now[tile][0], now[tile][2]

    lax.fori_loop(0, STEPS - 1, lambda k, _: (step(k, False), 0)[1], 0)
    step(STEPS - 1, True)


def finish(edge_coef, edge_field, saved, result, edge_wet, got1, got2, out, field, halo):
    even = lax.axis_index("lat") % 2 == 0
    lane, row = lanes(8), sublanes(8)
    for level in range(LEVELS):
        out[level, 8 : SIZE - 8, :] = result[level, 8 : SIZE - 8, :]
    for v in range(10):
        for tile in range(TILES):
            one, two = got1[v, tile], got2[v, tile]
            halo[v, 0, tile] = jnp.where(even, two, one)
            halo[v, 1, tile] = jnp.where(even, one, two)
    for side in range(2):
        tiles = [halo[9, side, tile] for tile in range(TILES)]
        for dc in (-1, 0, 1):
            for tile, x in enumerate(tiles if dc == 0 else shifted(tiles, dc, lane)):
                field[dc + 1, 3 * side, tile] = x
            for tile in range(TILES):
                field[dc + 1, 1 + side, tile] = edge_field[dc + 1, side, tile]

    for k in range(STEPS):
        new = [[], [], [], []]
        for tile in range(TILES):
            now = []
            for place in range(4):
                if place in (0, 3):
                    get = lambda c: halo[c, place // 3, tile]
                else:
                    get = lambda c: edge_coef[c, place - 1, tile]
                now.append(sums(get, [field[dc, place, tile] for dc in range(3)]))
            for place in range(4):
                before = (None, now[0][2], saved[k, 1, tile], now[2][2])[place]
                after = (now[1][0], saved[k, 0, tile], now[3][0], None)[place]
                new[place].append(
                    now[place][1] + north_of(before, now[place][2], row) + south_of(now[place][0], after, row)
                )
        if k < STEPS - 1:
            for place in range(4):
                for dc in (-1, 0, 1):
                    for tile, x in enumerate(new[place] if dc == 0 else shifted(new[place], dc, lane)):
                        field[dc + 1, place, tile] = x
        else:
            for side in range(2):
                rows = slice(0, 8) if side == 0 else slice(SIZE - 8, SIZE)
                for level in range(LEVELS):
                    x = turn(new[1 + side][level], -(16 * level + 8))
                    out[level, rows, :] = edge_wet[side, level] * x


VMEM = pl.BlockSpec(memory_space=pltpu.VMEM)


def call(body, args, outs, scratch=(), flops=1000000, near=True):
    kind = pltpu.VMEM if near else jax.ShapeDtypeStruct
    return pl.pallas_call(
        body,
        out_shape=[kind(shape, F32) for shape in outs],
        in_specs=[VMEM] * len(args),
        out_specs=[VMEM] * len(outs),
        scratch_shapes=[pltpu.VMEM(shape, F32) for shape in scratch],
        compiler_params=pltpu.CompilerParams(vmem_limit_bytes=40 * 1024 * 1024),
        cost_estimate=pl.CostEstimate(flops=flops, bytes_accessed=4 * 1024 * 1024, transcendentals=0),
        name=body.__name__,
    )(*args)


def shards(cotangent, coefficients, wet_mask):
    num_lon, num_lat = lax.axis_size("lon"), lax.axis_size("lat")

    def swap_lon(x, odd):
        pairs = [(i, ((i + odd) ^ 1) - odd) for i in range(num_lon)]
        return lax.ppermute(x, "lon", [(i, j % num_lon) for i, j in pairs])

    def swap_chip(x):
        return lax.ppermute(x, "lat", [(i, i ^ 1) for i in range(num_lat)])

    def swap_far(x):
        pairs = []
        for lon in range(num_lon):
            for lat in range(1, num_lat - 1):
                pairs.append((lon * num_lat + lat, lon * num_lat + ((lat + 1) ^ 1) - 1))
            pairs.append((lon * num_lat + num_lat - 1, (num_lon - 1 - lon) * num_lat + num_lat - 1))
        return lax.ppermute(x, ("lon", "lat"), pairs)

    fields = (cotangent, coefficients, wet_mask)
    lon1, lon2 = call(pack_lon, fields, [(320, SIZE)] * 2)
    got2 = swap_lon(lon2, 1)
    got1 = swap_lon(lon1, 0)
    main = call(rotate_main, fields + (lon1,), [(12, LEVELS, SIZE, SIZE)])[0]
    lat1, lat2 = call(pack_lat, (main, got1, got2), [(10, TILES, 8, SIZE)] * 2)
    far2 = swap_far(lat2)
    far1 = swap_chip(lat1)
    held = call(
        inner,
        (main, got1, got2, wet_mask, lat1),
        [(9, 2, TILES, 8, SIZE), (3, 2, TILES, 8, SIZE), (STEPS, 2, TILES, 8, SIZE), (LEVELS, SIZE, SIZE), (2, LEVELS, 8, SIZE)],
        [(9, TILES, SIZE, SIZE), (3, TILES, SIZE, SIZE)],
        flops=30000000,
    )
    return call(
        finish,
        tuple(held) + (far1, far2),
        [(LEVELS, SIZE, SIZE)],
        [(3, 4, TILES, 8, SIZE), (10, 2, TILES, 8, SIZE)],
        near=False,
    )[0]


def solution(mesh):
    in_specs = (P(None, "lat", "lon"), P(None, None, "lat", "lon"), P(None, "lat", "lon"))
    out_specs = P(None, "lat", "lon")
    return jax.shard_map(shards, mesh=mesh, in_specs=in_specs, out_specs=out_specs, check_vma=False)
```

```python
import jax
import jax.numpy as jnp
from jax import lax
from jax.experimental import pallas as pl
from jax.experimental.pallas import tpu as pltpu
from jax.sharding import PartitionSpec as P


STEPS = 8
LEVELS = 4
SIZE = 128
TILES = LEVELS + 1
F32 = jnp.float32
BF16 = jnp.bfloat16


def dc_of(c):
    return c % 3 - 1


def lanes(rows):
    return lax.broadcasted_iota(jnp.int32, (rows, SIZE), 1)


def sublanes(rows):
    return lax.broadcasted_iota(jnp.int32, (rows, SIZE), 0)


def turn(x, shift, axis=1):
    shift = shift % x.shape[axis]
    return x if shift == 0 else pltpu.roll(x, shift, axis)


def seam(level, dc):
    return 16 * level + (8 if dc == 1 else 7)


def join(mains, rim, dc, lane):
    if dc == 0:
        return list(mains) + [rim]
    fixed, new_rim = [], rim
    for level in range(LEVELS):
        here = lane == seam(level, dc)
        fixed.append(jnp.where(here, rim, mains[level]))
        new_rim = jnp.where(here, mains[level], new_rim)
    return fixed + [new_rim]


def shifted(tiles, dc, lane):
    return join([turn(t, dc) for t in tiles[:LEVELS]], turn(tiles[LEVELS], dc), dc, lane)


def edge_choices(choose):
    choose[...] = jnp.zeros_like(choose)
    cell, lane = sublanes(16), lanes(16)
    for block in range(16):
        value, level = block // LEVELS, block % LEVELS
        base = 64 * (value % 2) + 16 * level
        second = value >= 2
        at = lane - (base + (8 if second else 0))
        east = (cell >= 8) & (cell - 8 == at)
        at = lane - (base + (0 if second else 8))
        west = (cell < 8) & (cell == at)
        choose[SIZE * block + SIZE - 16 : SIZE * block + SIZE, :SIZE] = east.astype(F32).astype(BF16)
        choose[SIZE * block : SIZE * block + 16, SIZE:] = west.astype(F32).astype(BF16)


def column(v, level):
    return slice(SIZE * (LEVELS * v + level), SIZE * (LEVELS * v + level) + SIZE)


def pack_lon(cot_far, coef_far, wet_far, pay1, pay2, masked, cot, wet, coef, choose, sems):
    parts = [(0, 4), (4, 8), (8, 9)]
    copies = [pltpu.make_async_copy(wet_far, wet, sems.at[0])]
    for n, (start, stop) in enumerate(parts):
        copies.append(pltpu.make_async_copy(coef_far.at[start:stop], coef.at[start:stop], sems.at[1 + n]))
    copies.append(pltpu.make_async_copy(cot_far, cot, sems.at[4]))
    for copy in copies:
        copy.start()
    is_top = lax.axis_index("lat") == lax.axis_size("lat") - 1
    edge_choices(choose)

    copies[0].wait()
    sea = [wet[level].astype(F32).astype(BF16) for level in range(LEVELS)]
    for n, (start, stop) in enumerate(parts):
        copies[1 + n].wait()
        for v in range(start, stop):
            for level in range(LEVELS):
                masked[:, column(v, level)] = coef[v, level] * sea[level]
                if v >= 6:
                    rows = slice(SIZE - 16, SIZE)
                    here, other = coef[v, level, rows, :].astype(F32), coef[8 - v, level, rows, :].astype(F32)
                    here = jnp.where((sublanes(16) == 15) & is_top, other, here)
                    masked[rows, column(v, level)] = (here * wet[level, rows, :].astype(F32)).astype(BF16)
        if n < 2:
            both = jnp.dot(masked[:, 2048 * n : 2048 * n + 2048], choose[...], preferred_element_type=F32)
            east, west = both[:, :SIZE], both[:, SIZE:]
            pay1[SIZE * n : SIZE * n + SIZE, :] = east
            pay2[SIZE * n : SIZE * n + SIZE, :] = west

    lane = lanes(16)
    first = (lane & 8) == 0

    def both_edges(block):
        out = None
        for half in (0, 1):
            for level in range(LEVELS):
                rows = slice(16 * block, 16 * block + 16)
                x = cot[level, rows, :] if half else masked[rows, column(8, level)].astype(F32)
                x = turn(x, 64 * half + 16 * level + 8)
                out = x if out is None else jnp.where((lane >> 4) == 4 * half + level, x, out)
        return out

    copies[4].wait()
    for block in range(4):
        a, b = both_edges(block), both_edges(block + 4)
        row = 256 + 16 * block
        pay1[row : row + 16, :] = jnp.where(first, a, turn(b, 8))
        pay2[row : row + 16, :] = jnp.where(first, turn(b, -8), a)


def rotate_main(masked, cot, token, out):
    del token
    for block in range(8):
        rows = slice(16 * block, 16 * block + 16)
        for level in range(LEVELS):
            for v in range(9):
                out[v, level, rows, :] = turn(masked[rows, column(v, level)].astype(F32), 16 * level + 8 + dc_of(v))
            for dc in (-1, 0, 1):
                out[10 + dc, level, rows, :] = turn(cot[level, rows, :], 16 * level + 8 + dc)


def rims(got1, got2, start, count, lane):
    first = (lane & 8) == 0
    res = []
    for pair in range(5):
        if pair < 4:
            row, second = SIZE * (pair // 2) + start, pair % 2 == 1
        else:
            row, second = 256 + start % 64, start >= 64
        from_west, from_east = got1[row : row + count, :], got2[row : row + count, :]
        if second:
            from_west, from_east = turn(from_west, -8), turn(from_east, 8)
        res.append(jnp.where(first, from_west, from_east))
    return res


VALUES = [(c, dc_of(c)) for c in range(9)] + [(9, -1), (9, 0), (9, 1)]


def tiles_of(main, got1, got2, start, count, lane):
    rim_tiles = rims(got1, got2, start, count, lane)
    rows = slice(start, start + count)
    res = []
    for v, dc in VALUES:
        at = v if v < 9 else 10 + dc
        rim = turn(rim_tiles[v // 2], dc + 64 * (v % 2))
        res.append(join([main[at, level, rows, :] for level in range(LEVELS)], rim, dc, lane))
    return res


PAIRS = [(0, 1), (2, 3), (4, None), (8, 7), (6, 5)]
MIRRORED = [3, 4, 2, 0, 1, 5]
SENT = 27


def outgoing(built, northward, lane, row):
    near = (row >= 4) if northward else (row < 4)
    units = []
    for one, two in PAIRS:
        if two is None:
            units.append(built[one])
        else:
            units.append([jnp.where(near, built[one][t], turn(built[two][t], 4, 0)) for t in range(TILES)])
    field, added = built[9:], [jnp.zeros((8, SIZE), F32)] * TILES
    for k in range(4):
        new = []
        for t in range(TILES):
            down, level, up = sums(lambda c: built[c][t], [field[dc][t] for dc in range(3)])
            up, down = turn(up, 1, 0), turn(down, -1, 0)
            across = up if northward else down
            if northward:
                place_a, place_b = (0 if k == 0 else 4 - k), 7 - k
            else:
                place_a, place_b = (7 if k == 0 else k + 3), k
            a = across if k == 0 else turn(across, 4, 0)
            added[t] = jnp.where(row == place_a, a, jnp.where(row == place_b, level + across, added[t]))
            new.append(level + up + down)
        if k < 3:
            field = [shifted(new, -1, lane), new, shifted(new, 1, lane)]
    return units + [added]


def pack_lat(main, got1, got2, pay1, pay2):
    lat = lax.axis_index("lat")
    even = lat % 2 == 0
    is_top = lat == lax.axis_size("lat") - 1
    lane, row = lanes(8), sublanes(8)
    south = outgoing(tiles_of(main, got1, got2, 0, 8, lane), False, lane, row)
    north = outgoing(tiles_of(main, got1, got2, SIZE - 8, 8, lane), True, lane, row)

    def flat(units):
        res = [units[u][t] for u in range(6) for t in range(LEVELS)]
        return res + [jnp.where(lane < 64, units[u][LEVELS], turn(units[u + 1][LEVELS], 64)) for u in (0, 2, 4)]

    south_flat, north_flat = flat(south), flat(north)
    for n in range(SENT):
        pay1[n] = jnp.where(even, north_flat[n], south_flat[n])
        pay2[n] = jnp.where(even, south_flat[n], north_flat[n])

    @pl.when(is_top)
    def _():
        turned = [None] * 6
        for u in range(6):
            tiles = []
            for tile in range(TILES):
                index = (lane ^ 15) if tile == LEVELS else ((143 + 32 * tile - lane) & 127)
                x = jnp.take_along_axis(north[u][tile], index, axis=1, mode="promise_in_bounds")
                tiles.append(jnp.take_along_axis(x, 7 - row, axis=0, mode="promise_in_bounds"))
            turned[MIRRORED[u]] = tiles
        for n, x in enumerate(flat(turned)):
            pay2[n] = x


def sums(coef_tiles, field_tiles):
    res = []
    for dr in range(3):
        total = coef_tiles(3 * dr) * field_tiles[0]
        for dc in (1, 2):
            total = total + coef_tiles(3 * dr + dc) * field_tiles[dc]
        res.append(total)
    return res


def north_of(before, here, row):
    x = turn(here, 1, 0)
    return x if before is None else jnp.where(row == 0, turn(before, 1, 0), x)


def south_of(here, after, row):
    x = turn(here, -1, 0)
    return x if after is None else jnp.where(row == 7, turn(after, -1, 0), x)


def inner(main, got1, got2, wet, token, edge_coef, edge_field, saved, result, edge_wet, coef, field):
    del token
    lane16 = lanes(16)
    for block in range(8):
        rows = slice(16 * block, 16 * block + 16)
        built = tiles_of(main, got1, got2, 16 * block, 16, lane16)
        for v in range(12):
            for tile in range(TILES):
                x = built[v][tile]
                if v < 9:
                    coef[v, tile, rows, :] = x
                else:
                    field[v - 9, tile, rows, :] = x
                if block in (0, 7):
                    side, part = (0, x[:8]) if block == 0 else (1, x[8:])
                    if v < 9:
                        edge_coef[v, side, tile] = part
                    else:
                        edge_field[v - 9, side, tile] = part
    for level in range(LEVELS):
        edge_wet[0, level] = wet[level, :8, :].astype(F32)
        edge_wet[1, level] = wet[level, SIZE - 8 :, :].astype(F32)

    lane, row = lanes(8), sublanes(8)

    def step(k, last):
        done = [None] * TILES
        older = [[None] * TILES, [None] * TILES]
        for t in range(17):
            now = []
            for tile in range(TILES):
                if t < 16:
                    rows = slice(8 * t, 8 * t + 8)
                    now.append(sums(lambda c: coef[c, tile, rows, :], [field[dc, tile, rows, :] for dc in range(3)]))
            if t < 16:
                for tile in range(TILES):
                    if t == 1:
                        saved[k, 0, tile] = now[tile][0]
                    if t == 14:
                        saved[k, 1, tile] = now[tile][2]
            if t >= 1 and not (last and t - 1 in (0, 15)):
                new = []
                for tile in range(TILES):
                    after = now[tile][0] if t < 16 else None
                    new.append(done[tile] + south_of(older[0][tile], after, row))
                rows = slice(8 * (t - 1), 8 * t)
                if last:
                    for level in range(LEVELS):
                        mask = wet[level, rows, :].astype(F32)
                        result[level, rows, :] = mask * turn(new[level], -(16 * level + 8))
                else:
                    for dc in (-1, 0, 1):
                        for tile, x in enumerate(new if dc == 0 else shifted(new, dc, lane)):
                            field[dc + 1, tile, rows, :] = x
            if t < 16:
                for tile in range(TILES):
                    done[tile] = now[tile][1] + north_of(older[1][tile], now[tile][2], row)
                    older[0][tile], older[1][tile] = now[tile][0], now[tile][2]

    lax.fori_loop(0, STEPS - 1, lambda k, _: (step(k, False), 0)[1], 0)
    step(STEPS - 1, True)


def finish(edge_coef, edge_field, saved, result, edge_wet, got1, got2, out, field, halo, added):
    even = lax.axis_index("lat") % 2 == 0
    lane, row = lanes(8), sublanes(8)
    for level in range(LEVELS):
        out[level, 8 : SIZE - 8, :] = result[level, 8 : SIZE - 8, :]
    for side in range(2):
        near = (row >= 4) if side == 0 else (row < 4)
        got = [jnp.where(even, got2[n], got1[n]) if side == 0 else jnp.where(even, got1[n], got2[n]) for n in range(SENT)]
        for u in range(6):
            for tile in range(TILES):
                if tile < LEVELS:
                    x = got[LEVELS * u + tile]
                else:
                    x = turn(got[24 + u // 2], 64 * (u % 2))
                if u == 5:
                    added[side, tile] = x
                else:
                    one, two = PAIRS[u]
                    halo[one, side, tile] = jnp.where(near, x, 0.0)
                    if two is not None:
                        halo[two, side, tile] = jnp.where(near, turn(x, 4, 0), 0.0)
        for dc in range(3):
            for tile in range(TILES):
                field[dc, 1 + side, tile] = edge_field[dc, side, tile]

    zero = jnp.zeros((8, SIZE), F32)
    for k in range(STEPS):
        new = [[], [], [], []]
        for tile in range(TILES):
            now = []
            for place in range(4):
                if place in (0, 3):
                    get = lambda c: halo[c, place // 3, tile]
                else:
                    get = lambda c: edge_coef[c, place - 1, tile]
                if k == 0 and place in (0, 3):
                    now.append([zero] * 3)
                else:
                    now.append(sums(get, [field[dc, place, tile] for dc in range(3)]))
            total = []
            for place in range(4):
                before = (None, now[0][2], saved[k, 1, tile], now[2][2])[place]
                after = (now[1][0], saved[k, 0, tile], now[3][0], None)[place]
                total.append(now[place][1] + north_of(before, now[place][2], row) + south_of(now[place][0], after, row))
            if k < 4:
                low, high = added[0, tile], added[1, tile]
                total[0] = total[0] + jnp.where(row == 7 - k, low, 0.0)
                total[3] = total[3] + jnp.where(row == k, high, 0.0)
                if k == 0:
                    total[1] = total[1] + jnp.where(row == 0, low, 0.0)
                    total[2] = total[2] + jnp.where(row == 7, high, 0.0)
                else:
                    total[0] = total[0] + jnp.where(row == 8 - k, turn(low, 4, 0), 0.0)
                    total[3] = total[3] + jnp.where(row == k - 1, turn(high, 4, 0), 0.0)
            for place in range(4):
                new[place].append(total[place])
        if k < STEPS - 1:
            for place in range(4):
                for dc in (-1, 0, 1):
                    for tile, x in enumerate(new[place] if dc == 0 else shifted(new[place], dc, lane)):
                        field[dc + 1, place, tile] = x
        else:
            for side in range(2):
                rows = slice(0, 8) if side == 0 else slice(SIZE - 8, SIZE)
                for level in range(LEVELS):
                    x = turn(new[1 + side][level], -(16 * level + 8))
                    out[level, rows, :] = edge_wet[side, level] * x


VMEM = pl.BlockSpec(memory_space=pltpu.VMEM)


def call(body, args, outs, scratch=(), flops=1000000, near=True, far_args=False):
    kind = pltpu.VMEM if near else jax.ShapeDtypeStruct
    return pl.pallas_call(
        body,
        out_shape=[kind(*(out if isinstance(out[0], tuple) else (out, F32))) for out in outs],
        in_specs=[pl.BlockSpec(memory_space=pl.ANY) if far_args else VMEM] * len(args),
        out_specs=[VMEM] * len(outs),
        scratch_shapes=[pltpu.VMEM(shape, F32) if isinstance(shape, tuple) else shape for shape in scratch],
        compiler_params=pltpu.CompilerParams(vmem_limit_bytes=40 * 1024 * 1024),
        cost_estimate=pl.CostEstimate(flops=flops, bytes_accessed=4 * 1024 * 1024, transcendentals=0),
        name=body.__name__,
    )(*args)


def shards(cotangent, coefficients, wet_mask):
    num_lon, num_lat = lax.axis_size("lon"), lax.axis_size("lat")

    def shift_lon(x, by):
        return lax.ppermute(x, "lon", [(i, (i + by) % num_lon) for i in range(num_lon)])

    def swap_chip(x):
        return lax.ppermute(x, "lat", [(i, i ^ 1) for i in range(num_lat)])

    def swap_far(x):
        pairs = []
        for lon in range(num_lon):
            for lat in range(1, num_lat - 1):
                pairs.append((lon * num_lat + lat, lon * num_lat + ((lat + 1) ^ 1) - 1))
            pairs.append((lon * num_lat + num_lat - 1, (num_lon - 1 - lon) * num_lat + num_lat - 1))
        return lax.ppermute(x, ("lon", "lat"), pairs)

    fields = [pltpu.with_memory_space_constraint(x, pltpu.HBM) for x in (cotangent, coefficients, wet_mask)]
    whole = (LEVELS, SIZE, SIZE)
    lon1, lon2, masked, cot, wet = call(
        pack_lon,
        fields,
        [(320, SIZE), (320, SIZE), ((SIZE, 36 * SIZE), BF16), whole, (whole, jnp.int32)],
        [pltpu.VMEM((9,) + whole, BF16), pltpu.VMEM((16 * SIZE, 2 * SIZE), BF16), pltpu.SemaphoreType.DMA((5,))],
        far_args=True,
    )
    got1 = shift_lon(lon1, 1)
    got2 = shift_lon(lon2, -1)
    main = call(rotate_main, (masked, cot, lon1), [(12,) + whole])[0]
    lat1, lat2 = call(pack_lat, (main, got1, got2), [(SENT, 8, SIZE)] * 2)
    far2 = swap_far(lat2)
    far1 = swap_chip(lat1)
    held = call(
        inner,
        (main, got1, got2, wet, lat2),
        [(9, 2, TILES, 8, SIZE), (3, 2, TILES, 8, SIZE), (STEPS, 2, TILES, 8, SIZE), whole, (2, LEVELS, 8, SIZE)],
        [(9, TILES, SIZE, SIZE), (3, TILES, SIZE, SIZE)],
        flops=30000000,
    )
    return call(
        finish,
        tuple(held) + (far1, far2),
        [whole],
        [(3, 4, TILES, 8, SIZE), (9, 2, TILES, 8, SIZE), (2, TILES, 8, SIZE)],
        near=False,
    )[0]


def solution(mesh):
    in_specs = (P(None, "lat", "lon"), P(None, None, "lat", "lon"), P(None, "lat", "lon"))
    out_specs = P(None, "lat", "lon")
    return jax.shard_map(shards, mesh=mesh, in_specs=in_specs, out_specs=out_specs, check_vma=False)
```

```python
import jax
import jax.numpy as jnp
from jax import lax
from jax.experimental import pallas as pl
from jax.experimental.pallas import tpu as pltpu
from jax.sharding import PartitionSpec as P


STEPS = 8
LEVELS = 4
SIZE = 128
TILES = LEVELS + 1
F32 = jnp.float32
BF16 = jnp.bfloat16


def dc_of(c):
    return c % 3 - 1


def lanes(rows):
    return lax.broadcasted_iota(jnp.int32, (rows, SIZE), 1)


def sublanes(rows):
    return lax.broadcasted_iota(jnp.int32, (rows, SIZE), 0)


def turn(x, shift, axis=1):
    shift = shift % x.shape[axis]
    return x if shift == 0 else pltpu.roll(x, shift, axis)


def seam(level, dc):
    return 16 * level + (8 if dc == 1 else 7)


def join(mains, rim, dc, lane):
    if dc == 0:
        return list(mains) + [rim]
    fixed, new_rim = [], rim
    for level in range(LEVELS):
        here = lane == seam(level, dc)
        fixed.append(jnp.where(here, rim, mains[level]))
        new_rim = jnp.where(here, mains[level], new_rim)
    return fixed + [new_rim]


def shifted(tiles, dc, lane):
    return join([turn(t, dc) for t in tiles[:LEVELS]], turn(tiles[LEVELS], dc), dc, lane)


EAST_LENT = [((0, 1), 0, (0, 1)), ((2, 3), 3, (0, 1)), ((4, 5), 6, (0, 1)), ((6,), 1, (0,)), ((7,), 4, (0,))]
WEST_LENT = [((0, 1), 2, (6, 7)), ((2, 3), 5, (6, 7)), ((4,), 1, (7,)), ((5,), 4, (7,))]


def place(c, level, eastward):
    second = (c % 4 >= 2) == eastward
    return 64 * (c % 2) + 16 * level + (8 if second else 0)


def edge_choices(choose, part):
    choose[...] = jnp.zeros_like(choose)
    cell, lane = sublanes(16), lanes(16)
    for block in range(5 * LEVELS):
        value, level = block // LEVELS, block % LEVELS
        for eastward in (True, False):
            lent = EAST_LENT if eastward else WEST_LENT
            x = cell - 8 if eastward else cell
            hit = None
            if value < 4:
                c = 4 * part + value
                taken = [t for _, host, cells in lent if host == c for t in cells]
                hit = (x == lane - place(c, level, eastward)) & (x >= 0) & (x < 8)
                for t in taken:
                    hit = hit & (x != t)
            else:
                for cells, host, at in lent:
                    if host // 4 == part:
                        for one, t in zip(cells, at):
                            here = (x == one) & (lane == place(host, level, eastward) + t)
                            hit = here if hit is None else hit | here
            start = SIZE * block + (SIZE - 16 if eastward else 0)
            columns = slice(0, SIZE) if eastward else slice(SIZE, 2 * SIZE)
            choose[start : start + 16, columns] = hit.astype(F32).astype(BF16)


def column(v, level):
    return slice(SIZE * (LEVELS * v + level), SIZE * (LEVELS * v + level) + SIZE)


def pack_lon(cot_far, coef_far, wet_far, pay1, pay2, masked, cot, wet, coef, choose, sems):
    parts = [(8, 9), (0, 4), (4, 8)]
    copies = [pltpu.make_async_copy(wet_far, wet, sems.at[0])]
    for n, (start, stop) in enumerate(parts):
        copies.append(pltpu.make_async_copy(coef_far.at[start:stop], coef.at[start:stop], sems.at[1 + n]))
    copies.append(pltpu.make_async_copy(cot_far, cot, sems.at[4]))
    for copy in copies:
        copy.start()
    is_top = lax.axis_index("lat") == lax.axis_size("lat") - 1
    for part in range(2):
        edge_choices(choose.at[part], part)

    copies[0].wait()
    sea = [wet[level].astype(F32).astype(BF16) for level in range(LEVELS)]
    for n, (start, stop) in enumerate(parts):
        copies[1 + n].wait()
        for v in range(start, stop):
            for level in range(LEVELS):
                masked[:, column(v, level)] = coef[v, level] * sea[level]
        if n == 2:
            copies[4].wait()
        for v in range(6, 9) if n == 2 else ():
            for level in range(LEVELS):
                rows = slice(SIZE - 16, SIZE)
                here, other = coef[v, level, rows, :].astype(F32), coef[8 - v, level, rows, :].astype(F32)
                here = jnp.where((sublanes(16) == 15) & is_top, other, here)
                masked[rows, column(v, level)] = (here * wet[level, rows, :].astype(F32)).astype(BF16)
    for part in range(2):
        both = jnp.dot(masked[:, 2048 * part : 2048 * part + 2048], choose[part, :2048], preferred_element_type=F32)
        both = both + jnp.dot(masked[:, 4096:], choose[part, 2048:], preferred_element_type=F32)
        pay1[SIZE * part : SIZE * part + SIZE, :] = both[:, :SIZE]
        pay2[SIZE * part : SIZE * part + SIZE, :] = both[:, SIZE:]

    lane = lanes(16)
    first = (lane & 8) == 0

    def both_edges(start):
        out = None
        for level in range(LEVELS):
            x = turn(cot[level, start : start + 16, :], 16 * level + 8)
            out = x if out is None else jnp.where((lane >> 4) == level, x, out)
        return out

    for half in range(2):
        a, b, c, d = [both_edges(32 * n + 16 * half) for n in range(4)]
        a, b = jnp.where(lane < 64, a, turn(c, 64)), jnp.where(lane < 64, b, turn(d, 64))
        row = 256 + 16 * half
        pay1[row : row + 16, :] = jnp.where(first, a, turn(b, 8))
        pay2[row : row + 16, :] = jnp.where(first, turn(b, -8), a)


def rotate_main(masked, cot, token, out):
    del token
    for block in range(8):
        rows = slice(16 * block, 16 * block + 16)
        for level in range(LEVELS):
            for v in range(9):
                out[v, level, rows, :] = turn(masked[rows, column(v, level)].astype(F32), 16 * level + 8 + dc_of(v))
            for dc in (-1, 0, 1):
                out[10 + dc, level, rows, :] = turn(cot[level, rows, :], 16 * level + 8 + dc)


def rims(got1, got2, start, count, lane):
    first = (lane & 8) == 0
    parts = [(got1[row : row + count, :], got2[row : row + count, :]) for row in (start, SIZE + start)]
    res = []
    for pair in range(4):
        from_west, from_east = parts[pair // 2]
        if pair % 2 == 1:
            from_west, from_east = turn(from_west, -8), turn(from_east, 8)
        res.append(jnp.where(first, from_west, from_east))
    row, n = 256 + start % 32, start // 32
    shift = 64 - 64 * (n // 2)
    from_west = turn(got1[row : row + count, :], shift - 8 * (n % 2))
    from_east = turn(got2[row : row + count, :], shift + 8 * (n % 2))
    last = jnp.where(first, from_west, from_east)
    for side, lent in ((0, EAST_LENT), (1, WEST_LENT)):
        for cells, host, at in lent:
            target = cells[0] + 8 * side
            x = turn(parts[host // 4][side], target - place(host, 0, side == 0) - at[0])
            within = (lane & 15) - target
            last = jnp.where((lane < 64) & (within >= 0) & (within < len(cells)), x, last)
    return res + [last]


VALUES = [(c, dc_of(c)) for c in range(9)] + [(9, -1), (9, 0), (9, 1)]


def tiles_of(main, got1, got2, start, count, lane):
    rim_tiles = rims(got1, got2, start, count, lane)
    rows = slice(start, start + count)
    res = []
    for v, dc in VALUES:
        at = v if v < 9 else 10 + dc
        rim = turn(rim_tiles[v // 2], dc + 64 * (v % 2))
        res.append(join([main[at, level, rows, :] for level in range(LEVELS)], rim, dc, lane))
    return res


PAIRS = [(0, 1), (2, 3), (8, 7), (6, 5)]
MIRRORED = [2, 3, 0, 1, 4]
MIDDLE = {True: [(1, 0, True), (2, 0, False), (3, 1, True)], False: [(1, 2, True), (2, 2, False), (3, 3, True)]}
UNITS = 5
SENT = 23


def ring_row(ring, northward):
    return 8 - ring if northward else ring - 1


def middle_row(near, northward):
    return (ring_row(4, northward) + (0 if near else 4)) % 8


def outgoing(built, northward, lane, row):
    near = (row >= 4) if northward else (row < 4)
    units = []
    for one, two in PAIRS:
        units.append([jnp.where(near, built[one][t], turn(built[two][t], 4, 0)) for t in range(TILES)])
    for ring, u, in_near in MIDDLE[northward]:
        at = middle_row(in_near, northward)
        for t in range(TILES):
            units[u][t] = jnp.where(row == at, turn(built[4][t], at - ring_row(ring, northward), 0), units[u][t])
    field, added = built[9:], [jnp.zeros((8, SIZE), F32)] * TILES
    for k in range(4):
        new = []
        for t in range(TILES):
            down, level, up = sums(lambda c: built[c][t], [field[dc][t] for dc in range(3)])
            up, down = turn(up, 1, 0), turn(down, -1, 0)
            across = up if northward else down
            if northward:
                place_a, place_b = (0 if k == 0 else 4 - k), 7 - k
            else:
                place_a, place_b = (7 if k == 0 else k + 3), k
            a = across if k == 0 else turn(across, 4, 0)
            added[t] = jnp.where(row == place_a, a, jnp.where(row == place_b, level + across, added[t]))
            new.append(level + up + down)
        if k < 3:
            field = [shifted(new, -1, lane), new, shifted(new, 1, lane)]
    return units + [added]


def pack_lat(main, got1, got2, pay1, pay2):
    lat = lax.axis_index("lat")
    even = lat % 2 == 0
    is_top = lat == lax.axis_size("lat") - 1
    lane, row = lanes(8), sublanes(8)
    south = outgoing(tiles_of(main, got1, got2, 0, 8, lane), False, lane, row)
    north = outgoing(tiles_of(main, got1, got2, SIZE - 8, 8, lane), True, lane, row)

    def flat(units):
        res = [units[u][t] for u in range(UNITS) for t in range(LEVELS)]
        rim = [unit[LEVELS] for unit in units]
        return res + [jnp.where(lane < 64, rim[0], turn(rim[1], 64)), jnp.where(lane < 64, rim[2], turn(rim[3], 64)), rim[4]]

    south_flat, north_flat = flat(south), flat(north)
    for n in range(SENT):
        pay1[n] = jnp.where(even, north_flat[n], south_flat[n])
        pay2[n] = jnp.where(even, south_flat[n], north_flat[n])

    @pl.when(is_top)
    def _():
        turned = [None] * UNITS
        for u in range(UNITS):
            tiles = []
            for tile in range(TILES):
                index = (lane ^ 15) if tile == LEVELS else ((143 + 32 * tile - lane) & 127)
                x = jnp.take_along_axis(north[u][tile], index, axis=1, mode="promise_in_bounds")
                tiles.append(jnp.take_along_axis(x, 7 - row, axis=0, mode="promise_in_bounds"))
            turned[MIRRORED[u]] = tiles
        for n, x in enumerate(flat(turned)):
            pay2[n] = x


def sums(coef_tiles, field_tiles):
    res = []
    for dr in range(3):
        total = coef_tiles(3 * dr) * field_tiles[0]
        for dc in (1, 2):
            total = total + coef_tiles(3 * dr + dc) * field_tiles[dc]
        res.append(total)
    return res


def north_of(before, here, row):
    return turn(here if before is None else jnp.where(row == 7, before, here), 1, 0)


def south_of(here, after, row):
    return turn(here if after is None else jnp.where(row == 0, after, here), -1, 0)


def inner(main, got1, got2, wet, token, edge_coef, edge_field, saved, result, edge_wet, coef, field, other):
    del token
    lane16 = lanes(16)
    for block in range(8):
        rows = slice(16 * block, 16 * block + 16)
        built = tiles_of(main, got1, got2, 16 * block, 16, lane16)
        for v in range(12):
            for tile in range(TILES):
                x = built[v][tile]
                if v < 9:
                    if dc_of(v) != 0 or tile == LEVELS:
                        coef[v, tile, rows, :] = x
                else:
                    field[v - 9, tile, rows, :] = x
                if block in (0, 7):
                    side, part = (0, x[:8]) if block == 0 else (1, x[8:])
                    if v < 9:
                        edge_coef[v, side, tile] = part
                    else:
                        edge_field[v - 9, side, tile] = part
    for level in range(LEVELS):
        edge_wet[0, level] = wet[level, :8, :].astype(F32)
        edge_wet[1, level] = wet[level, SIZE - 8 :, :].astype(F32)

    lane, row = lanes(8), sublanes(8)

    def weight(c, tile, rows):
        return main[c, tile, rows, :] if dc_of(c) == 0 and tile < LEVELS else coef[c, tile, rows, :]

    def step(k, last, field, other):
        done = [None] * TILES
        older = [[None] * TILES, [None] * TILES]
        for t in range(17):
            now = []
            for tile in range(TILES):
                if t < 16:
                    rows = slice(8 * t, 8 * t + 8)
                    now.append(sums(lambda c: weight(c, tile, rows), [field[dc, tile, rows, :] for dc in range(3)]))
            if t < 16:
                for tile in range(TILES):
                    if t == 1:
                        saved[k, 0, tile] = now[tile][0]
                    if t == 14:
                        saved[k, 1, tile] = now[tile][2]
            if t >= 1 and not (last and t - 1 in (0, 15)):
                new = []
                for tile in range(TILES):
                    after = now[tile][0] if t < 16 else None
                    new.append(done[tile] + south_of(older[0][tile], after, row))
                rows = slice(8 * (t - 1), 8 * t)
                if last:
                    for level in range(LEVELS):
                        mask = wet[level, rows, :].astype(F32)
                        result[level, rows, :] = mask * turn(new[level], -(16 * level + 8))
                else:
                    for dc in (-1, 0, 1):
                        for tile, x in enumerate(new if dc == 0 else shifted(new, dc, lane)):
                            other[dc + 1, tile, rows, :] = x
            if t < 16:
                for tile in range(TILES):
                    done[tile] = now[tile][1] + north_of(older[1][tile], now[tile][2], row)
                    older[0][tile], older[1][tile] = now[tile][0], now[tile][2]

    def two_steps(n, carry):
        step(2 * n, False, field, other)
        step(2 * n + 1, False, other, field)
        return carry

    lax.fori_loop(0, STEPS // 2 - 1, two_steps, 0)
    step(STEPS - 2, False, field, other)
    step(STEPS - 1, True, other, field)


def finish(edge_coef, edge_field, saved, result, edge_wet, got1, got2, out, field, halo, added):
    even = lax.axis_index("lat") % 2 == 0
    lane, row = lanes(8), sublanes(8)
    for level in range(LEVELS):
        out[level, 8 : SIZE - 8, :] = result[level, 8 : SIZE - 8, :]
    for side in range(2):
        near = (row >= 4) if side == 0 else (row < 4)
        got = [jnp.where(even, got2[n], got1[n]) if side == 0 else jnp.where(even, got1[n], got2[n]) for n in range(SENT)]
        northward = side == 0
        for tile in range(TILES):
            if tile < LEVELS:
                units = [got[LEVELS * u + tile] for u in range(UNITS)]
            else:
                units = [turn(got[LEVELS * UNITS + u // 2], 64 * (u % 2)) for u in range(UNITS)]
            added[side, tile] = units[4]
            for u, (one, two) in enumerate(PAIRS):
                halo[one, side, tile] = jnp.where(near, units[u], 0.0)
                halo[two, side, tile] = jnp.where(near, turn(units[u], 4, 0), 0.0)
            middle = jnp.zeros((8, SIZE), F32)
            for ring, u, in_near in MIDDLE[northward]:
                to = ring_row(ring, northward)
                middle = jnp.where(row == to, turn(units[u], to - middle_row(in_near, northward), 0), middle)
            halo[4, side, tile] = middle
        for dc in range(3):
            for tile in range(TILES):
                field[dc, 1 + side, tile] = edge_field[dc, side, tile]

    zero = jnp.zeros((8, SIZE), F32)
    for k in range(STEPS):
        new = [[], [], [], []]
        for tile in range(TILES):
            now = []
            for place in range(4):
                if place in (0, 3):
                    get = lambda c: halo[c, place // 3, tile]
                else:
                    get = lambda c: edge_coef[c, place - 1, tile]
                if k == 0 and place in (0, 3):
                    now.append([zero] * 3)
                else:
                    now.append(sums(get, [field[dc, place, tile] for dc in range(3)]))
            total = []
            for place in range(4):
                before = (None, now[0][2], saved[k, 1, tile], now[2][2])[place]
                after = (now[1][0], saved[k, 0, tile], now[3][0], None)[place]
                total.append(now[place][1] + north_of(before, now[place][2], row) + south_of(now[place][0], after, row))
            if k < 4:
                low, high = added[0, tile], added[1, tile]
                total[0] = total[0] + jnp.where(row == 7 - k, low, 0.0)
                total[3] = total[3] + jnp.where(row == k, high, 0.0)
                if k == 0:
                    total[1] = total[1] + jnp.where(row == 0, low, 0.0)
                    total[2] = total[2] + jnp.where(row == 7, high, 0.0)
                else:
                    total[0] = total[0] + jnp.where(row == 8 - k, turn(low, 4, 0), 0.0)
                    total[3] = total[3] + jnp.where(row == k - 1, turn(high, 4, 0), 0.0)
            for place in range(4):
                new[place].append(total[place])
        if k < STEPS - 1:
            for place in range(4):
                for dc in (-1, 0, 1):
                    for tile, x in enumerate(new[place] if dc == 0 else shifted(new[place], dc, lane)):
                        field[dc + 1, place, tile] = x
        else:
            for side in range(2):
                rows = slice(0, 8) if side == 0 else slice(SIZE - 8, SIZE)
                for level in range(LEVELS):
                    x = turn(new[1 + side][level], -(16 * level + 8))
                    out[level, rows, :] = edge_wet[side, level] * x


VMEM = pl.BlockSpec(memory_space=pltpu.VMEM)


def call(body, args, outs, scratch=(), flops=1000000, near=True, far_args=False):
    kind = pltpu.VMEM if near else jax.ShapeDtypeStruct
    return pl.pallas_call(
        body,
        out_shape=[kind(*(out if isinstance(out[0], tuple) else (out, F32))) for out in outs],
        in_specs=[pl.BlockSpec(memory_space=pl.ANY) if far_args else VMEM] * len(args),
        out_specs=[VMEM] * len(outs),
        scratch_shapes=[pltpu.VMEM(shape, F32) if isinstance(shape, tuple) else shape for shape in scratch],
        compiler_params=pltpu.CompilerParams(vmem_limit_bytes=40 * 1024 * 1024),
        cost_estimate=pl.CostEstimate(flops=flops, bytes_accessed=4 * 1024 * 1024, transcendentals=0),
        name=body.__name__,
    )(*args)


def shards(cotangent, coefficients, wet_mask):
    num_lon, num_lat = lax.axis_size("lon"), lax.axis_size("lat")

    def shift_lon(x, by):
        return lax.ppermute(x, "lon", [(i, (i + by) % num_lon) for i in range(num_lon)])

    def swap_chip(x):
        return lax.ppermute(x, "lat", [(i, i ^ 1) for i in range(num_lat)])

    def swap_far(x):
        pairs = []
        for lon in range(num_lon):
            for lat in range(1, num_lat - 1):
                pairs.append((lon * num_lat + lat, lon * num_lat + ((lat + 1) ^ 1) - 1))
            pairs.append((lon * num_lat + num_lat - 1, (num_lon - 1 - lon) * num_lat + num_lat - 1))
        return lax.ppermute(x, ("lon", "lat"), pairs)

    fields = [pltpu.with_memory_space_constraint(x, pltpu.HBM) for x in (cotangent, coefficients, wet_mask)]
    whole = (LEVELS, SIZE, SIZE)
    lon1, lon2, masked, cot, wet = call(
        pack_lon,
        fields,
        [(288, SIZE), (288, SIZE), ((SIZE, 36 * SIZE), BF16), whole, (whole, jnp.int32)],
        [pltpu.VMEM((9,) + whole, BF16), pltpu.VMEM((2, 20 * SIZE, 2 * SIZE), BF16), pltpu.SemaphoreType.DMA((5,))],
        far_args=True,
    )
    got1 = shift_lon(lon1, 1)
    got2 = shift_lon(lon2, -1)
    main = call(rotate_main, (masked, cot, lon1), [(12,) + whole])[0]
    lat1, lat2 = call(pack_lat, (main, got1, got2), [(SENT, 8, SIZE)] * 2)
    far2 = swap_far(lat2)
    far1 = swap_chip(lat1)
    held = call(
        inner,
        (main, got1, got2, wet, lat2),
        [(9, 2, TILES, 8, SIZE), (3, 2, TILES, 8, SIZE), (STEPS, 2, TILES, 8, SIZE), whole, (2, LEVELS, 8, SIZE)],
        [(9, TILES, SIZE, SIZE), (3, TILES, SIZE, SIZE), (3, TILES, SIZE, SIZE)],
        flops=30000000,
    )
    return call(
        finish,
        tuple(held) + (far1, far2),
        [whole],
        [(3, 4, TILES, 8, SIZE), (9, 2, TILES, 8, SIZE), (2, TILES, 8, SIZE)],
        near=False,
    )[0]


def solution(mesh):
    in_specs = (P(None, "lat", "lon"), P(None, None, "lat", "lon"), P(None, "lat", "lon"))
    out_specs = P(None, "lat", "lon")
    return jax.shard_map(shards, mesh=mesh, in_specs=in_specs, out_specs=out_specs, check_vma=False)
```

```python
import jax
import jax.numpy as jnp
from jax import lax
from jax.experimental import pallas as pl
from jax.experimental.pallas import tpu as pltpu
from jax.sharding import PartitionSpec as P


STEPS = 8
LEVELS = 4
SIZE = 128
TILES = LEVELS + 1
F32 = jnp.float32
BF16 = jnp.bfloat16


def dc_of(c):
    return c % 3 - 1


def lanes(rows):
    return lax.broadcasted_iota(jnp.int32, (rows, SIZE), 1)


def sublanes(rows):
    return lax.broadcasted_iota(jnp.int32, (rows, SIZE), 0)


def turn(x, shift, axis=1):
    shift = shift % x.shape[axis]
    return x if shift == 0 else pltpu.roll(x, shift, axis)


def seam(level, dc):
    return 16 * level + (8 if dc == 1 else 7)


def join(mains, rim, dc, lane):
    if dc == 0:
        return list(mains) + [rim]
    fixed, new_rim = [], rim
    for level in range(LEVELS):
        here = lane == seam(level, dc)
        fixed.append(jnp.where(here, rim, mains[level]))
        new_rim = jnp.where(here, mains[level], new_rim)
    return fixed + [new_rim]


def shifted(tiles, dc, lane):
    return join([turn(t, dc) for t in tiles[:LEVELS]], turn(tiles[LEVELS], dc), dc, lane)


EAST_LENT = [((0, 1), 0, (0, 1)), ((2, 3), 3, (0, 1)), ((4, 5), 6, (0, 1)), ((6,), 1, (0,)), ((7,), 4, (0,))]
WEST_LENT = [((0, 1), 2, (6, 7)), ((2, 3), 5, (6, 7)), ((4,), 1, (7,)), ((5,), 4, (7,))]


def place(c, level, eastward):
    second = (c % 4 >= 2) == eastward
    return 64 * (c % 2) + 16 * level + (8 if second else 0)


def edge_choices(choose, part):
    choose[...] = jnp.zeros_like(choose)
    cell, lane = sublanes(16), lanes(16)
    for block in range(5 * LEVELS):
        value, level = block // LEVELS, block % LEVELS
        for eastward in (True, False):
            lent = EAST_LENT if eastward else WEST_LENT
            x = cell - 8 if eastward else cell
            hit = None
            if value < 4:
                c = 4 * part + value
                taken = [t for _, host, cells in lent if host == c for t in cells]
                hit = (x == lane - place(c, level, eastward)) & (x >= 0) & (x < 8)
                for t in taken:
                    hit = hit & (x != t)
            else:
                for cells, host, at in lent:
                    if host // 4 == part:
                        for one, t in zip(cells, at):
                            here = (x == one) & (lane == place(host, level, eastward) + t)
                            hit = here if hit is None else hit | here
            start = SIZE * block + (SIZE - 16 if eastward else 0)
            columns = slice(0, SIZE) if eastward else slice(SIZE, 2 * SIZE)
            choose[start : start + 16, columns] = hit.astype(F32).astype(BF16)


def column(v, level):
    return slice(SIZE * (LEVELS * v + level), SIZE * (LEVELS * v + level) + SIZE)


def pack_lon(cot_far, coef_far, wet_far, pay1, pay2, masked, cot, wet, coef, choose, sems):
    parts = [(8, 9), (0, 4), (4, 8)]
    copies = [pltpu.make_async_copy(wet_far, wet, sems.at[0])]
    for n, (start, stop) in enumerate(parts):
        copies.append(pltpu.make_async_copy(coef_far.at[start:stop], coef.at[start:stop], sems.at[1 + n]))
    copies.append(pltpu.make_async_copy(cot_far, cot, sems.at[4]))
    for copy in copies:
        copy.start()
    is_top = lax.axis_index("lat") == lax.axis_size("lat") - 1
    for part in range(2):
        edge_choices(choose.at[part], part)

    copies[0].wait()
    sea = [wet[level].astype(F32).astype(BF16) for level in range(LEVELS)]
    for n, (start, stop) in enumerate(parts):
        copies[1 + n].wait()
        for v in range(start, stop):
            for level in range(LEVELS):
                masked[:, column(v, level)] = coef[v, level] * sea[level]
        if n == 2:
            copies[4].wait()
        for v in range(6, 9) if n == 2 else ():
            for level in range(LEVELS):
                rows = slice(SIZE - 16, SIZE)
                here, other = coef[v, level, rows, :].astype(F32), coef[8 - v, level, rows, :].astype(F32)
                here = jnp.where((sublanes(16) == 15) & is_top, other, here)
                masked[rows, column(v, level)] = (here * wet[level, rows, :].astype(F32)).astype(BF16)
    for part in range(2):
        both = jnp.dot(masked[:, 2048 * part : 2048 * part + 2048], choose[part, :2048], preferred_element_type=F32)
        both = both + jnp.dot(masked[:, 4096:], choose[part, 2048:], preferred_element_type=F32)
        pay1[SIZE * part : SIZE * part + SIZE, :] = both[:, :SIZE]
        pay2[SIZE * part : SIZE * part + SIZE, :] = both[:, SIZE:]

    lane = lanes(16)
    first = (lane & 8) == 0

    def both_edges(start):
        out = None
        for level in range(LEVELS):
            x = turn(cot[level, start : start + 16, :], 16 * level + 8)
            out = x if out is None else jnp.where((lane >> 4) == level, x, out)
        return out

    for half in range(2):
        a, b, c, d = [both_edges(32 * n + 16 * half) for n in range(4)]
        a, b = jnp.where(lane < 64, a, turn(c, 64)), jnp.where(lane < 64, b, turn(d, 64))
        row = 256 + 16 * half
        pay1[row : row + 16, :] = jnp.where(first, a, turn(b, 8))
        pay2[row : row + 16, :] = jnp.where(first, turn(b, -8), a)


def rotate_main(masked, cot, token, out):
    del token
    for block in range(8):
        rows = slice(16 * block, 16 * block + 16)
        for level in range(LEVELS):
            for v in range(9):
                out[v, level, rows, :] = turn(masked[rows, column(v, level)].astype(F32), 16 * level + 8 + dc_of(v))
            for dc in (-1, 0, 1):
                out[10 + dc, level, rows, :] = turn(cot[level, rows, :], 16 * level + 8 + dc)


def rims(got1, got2, start, count, lane):
    first = (lane & 8) == 0
    parts = [(got1[row : row + count, :], got2[row : row + count, :]) for row in (start, SIZE + start)]
    res = []
    for pair in range(4):
        from_west, from_east = parts[pair // 2]
        if pair % 2 == 1:
            from_west, from_east = turn(from_west, -8), turn(from_east, 8)
        res.append(jnp.where(first, from_west, from_east))
    row, n = 256 + start % 32, start // 32
    shift = 64 - 64 * (n // 2)
    from_west = turn(got1[row : row + count, :], shift - 8 * (n % 2))
    from_east = turn(got2[row : row + count, :], shift + 8 * (n % 2))
    last = jnp.where(first, from_west, from_east)
    for side, lent in ((0, EAST_LENT), (1, WEST_LENT)):
        for cells, host, at in lent:
            target = cells[0] + 8 * side
            x = turn(parts[host // 4][side], target - place(host, 0, side == 0) - at[0])
            within = (lane & 15) - target
            last = jnp.where((lane < 64) & (within >= 0) & (within < len(cells)), x, last)
    return res + [last]


VALUES = [(c, dc_of(c)) for c in range(9)] + [(9, -1), (9, 0), (9, 1)]


def tiles_of(main, got1, got2, start, count, lane):
    rim_tiles = rims(got1, got2, start, count, lane)
    rows = slice(start, start + count)
    res = []
    for v, dc in VALUES:
        at = v if v < 9 else 10 + dc
        rim = turn(rim_tiles[v // 2], dc + 64 * (v % 2))
        res.append(join([main[at, level, rows, :] for level in range(LEVELS)], rim, dc, lane))
    return res


PAIRS = [(0, 1), (2, 3), (8, 7), (6, 5)]
MIRRORED = [2, 3, 0, 1, 4]
MIDDLE = {True: [(1, 0, True), (2, 0, False), (3, 1, True)], False: [(1, 2, True), (2, 2, False), (3, 3, True)]}
UNITS = 5
SENT = 23


def ring_row(ring, northward):
    return 8 - ring if northward else ring - 1


def middle_row(near, northward):
    return (ring_row(4, northward) + (0 if near else 4)) % 8


def outgoing(built, northward, lane, row):
    near = (row >= 4) if northward else (row < 4)
    units = []
    for one, two in PAIRS:
        units.append([jnp.where(near, built[one][t], turn(built[two][t], 4, 0)) for t in range(TILES)])
    for ring, u, in_near in MIDDLE[northward]:
        at = middle_row(in_near, northward)
        for t in range(TILES):
            units[u][t] = jnp.where(row == at, turn(built[4][t], at - ring_row(ring, northward), 0), units[u][t])
    field, added = built[9:], [jnp.zeros((8, SIZE), F32)] * TILES
    for k in range(4):
        new = []
        for t in range(TILES):
            down, level, up = sums(lambda c: built[c][t], [field[dc][t] for dc in range(3)])
            up, down = turn(up, 1, 0), turn(down, -1, 0)
            across = up if northward else down
            if northward:
                place_a, place_b = (0 if k == 0 else 4 - k), 7 - k
            else:
                place_a, place_b = (7 if k == 0 else k + 3), k
            a = across if k == 0 else turn(across, 4, 0)
            added[t] = jnp.where(row == place_a, a, jnp.where(row == place_b, level + across, added[t]))
            new.append(level + up + down)
        if k < 3:
            field = [shifted(new, -1, lane), new, shifted(new, 1, lane)]
    return units + [added]


def pack_lat(main, got1, got2, pay1, pay2):
    lat = lax.axis_index("lat")
    even = lat % 2 == 0
    is_top = lat == lax.axis_size("lat") - 1
    lane, row = lanes(8), sublanes(8)
    south = outgoing(tiles_of(main, got1, got2, 0, 8, lane), False, lane, row)
    north = outgoing(tiles_of(main, got1, got2, SIZE - 8, 8, lane), True, lane, row)

    def flat(units):
        res = [units[u][t] for u in range(UNITS) for t in range(LEVELS)]
        rim = [unit[LEVELS] for unit in units]
        return res + [jnp.where(lane < 64, rim[0], turn(rim[1], 64)), jnp.where(lane < 64, rim[2], turn(rim[3], 64)), rim[4]]

    south_flat, north_flat = flat(south), flat(north)
    for n in range(SENT):
        pay1[n] = jnp.where(even, north_flat[n], south_flat[n])
        pay2[n] = jnp.where(even, south_flat[n], north_flat[n])

    @pl.when(is_top)
    def _():
        turned = [None] * UNITS
        for u in range(UNITS):
            tiles = []
            for tile in range(TILES):
                index = (lane ^ 15) if tile == LEVELS else ((143 + 32 * tile - lane) & 127)
                x = jnp.take_along_axis(north[u][tile], index, axis=1, mode="promise_in_bounds")
                tiles.append(jnp.take_along_axis(x, 7 - row, axis=0, mode="promise_in_bounds"))
            turned[MIRRORED[u]] = tiles
        for n, x in enumerate(flat(turned)):
            pay2[n] = x


def sums(coef_tiles, field_tiles):
    res = []
    for dr in range(3):
        total = coef_tiles(3 * dr) * field_tiles[0]
        for dc in (1, 2):
            total = total + coef_tiles(3 * dr + dc) * field_tiles[dc]
        res.append(total)
    return res


def north_of(before, here, row):
    return turn(here if before is None else jnp.where(row == here.shape[0] - 1, before, here), 1, 0)


def south_of(here, after, row):
    return turn(here if after is None else jnp.where(row == 0, after, here), -1, 0)


def inner(main, got1, got2, wet, token, edge_coef, edge_field, saved, result, edge_wet, coef, field, other):
    del token
    lane16 = lanes(16)
    for block in range(8):
        rows = slice(16 * block, 16 * block + 16)
        built = tiles_of(main, got1, got2, 16 * block, 16, lane16)
        for v in range(12):
            for tile in range(TILES):
                x = built[v][tile]
                if v < 9:
                    if dc_of(v) != 0 or tile == LEVELS:
                        coef[v, tile, rows, :] = x
                else:
                    field[v - 9, tile, rows, :] = x
                if block in (0, 7):
                    side, part = (0, x[:8]) if block == 0 else (1, x[8:])
                    if v < 9:
                        edge_coef[v, side, tile] = part
                    else:
                        edge_field[v - 9, side, tile] = part
    for level in range(LEVELS):
        edge_wet[0, level] = wet[level, :8, :].astype(F32)
        edge_wet[1, level] = wet[level, SIZE - 8 :, :].astype(F32)

    lane, row = lane16, sublanes(16)

    def weight(c, tile, rows):
        return main[c, tile, rows, :] if dc_of(c) == 0 and tile < LEVELS else coef[c, tile, rows, :]

    def step(k, last, field, other):
        done, older = [None] * TILES, [[None] * TILES, [None] * TILES]
        for t in range(9):
            now = []
            if t < 8:
                rows = slice(16 * t, 16 * t + 16)
                for tile in range(TILES):
                    now.append(sums(lambda c: weight(c, tile, rows), [field[dc, tile, rows, :] for dc in range(3)]))
                    if t == 0:
                        saved[k, 0, tile] = now[tile][0][8:]
                    if t == 7:
                        saved[k, 1, tile] = now[tile][2][:8]
            if t >= 1:
                new = []
                for tile in range(TILES):
                    after = now[tile][0] if t < 8 else None
                    new.append(done[tile] + south_of(older[0][tile], after, row))
                rows = slice(16 * (t - 1), 16 * t)
                if last:
                    for level in range(LEVELS):
                        mask = wet[level, rows, :].astype(F32)
                        result[level, rows, :] = mask * turn(new[level], -(16 * level + 8))
                else:
                    for dc in (-1, 0, 1):
                        for tile, x in enumerate(new if dc == 0 else shifted(new, dc, lane)):
                            other[dc + 1, tile, rows, :] = x
            if t < 8:
                for tile in range(TILES):
                    done[tile] = now[tile][1] + north_of(older[1][tile], now[tile][2], row)
                    older[0][tile], older[1][tile] = now[tile][0], now[tile][2]

    def two_steps(n, carry):
        step(2 * n, False, field, other)
        step(2 * n + 1, False, other, field)
        return carry

    lax.fori_loop(0, STEPS // 2 - 1, two_steps, 0)
    step(STEPS - 2, False, field, other)
    step(STEPS - 1, True, other, field)


def finish(edge_coef, edge_field, saved, result, edge_wet, both, got2, out, field, halo, added):
    lat = lax.axis_index("lat")
    even = lat % 2 == 0
    got1 = both.at[1 - lat % 2]
    lane, row = lanes(8), sublanes(8)
    for level in range(LEVELS):
        out[level, 8 : SIZE - 8, :] = result[level, 8 : SIZE - 8, :]
    for side in range(2):
        near = (row >= 4) if side == 0 else (row < 4)
        got = [jnp.where(even, got2[n], got1[n]) if side == 0 else jnp.where(even, got1[n], got2[n]) for n in range(SENT)]
        northward = side == 0
        for tile in range(TILES):
            if tile < LEVELS:
                units = [got[LEVELS * u + tile] for u in range(UNITS)]
            else:
                units = [turn(got[LEVELS * UNITS + u // 2], 64 * (u % 2)) for u in range(UNITS)]
            added[side, tile] = units[4]
            for u, (one, two) in enumerate(PAIRS):
                halo[one, side, tile] = jnp.where(near, units[u], 0.0)
                halo[two, side, tile] = jnp.where(near, turn(units[u], 4, 0), 0.0)
            middle = jnp.zeros((8, SIZE), F32)
            for ring, u, in_near in MIDDLE[northward]:
                to = ring_row(ring, northward)
                middle = jnp.where(row == to, turn(units[u], to - middle_row(in_near, northward), 0), middle)
            halo[4, side, tile] = middle
        for dc in range(3):
            for tile in range(TILES):
                field[dc, 1 + side, tile] = edge_field[dc, side, tile]

    zero = jnp.zeros((8, SIZE), F32)
    for k in range(STEPS):
        new = [[], [], [], []]
        for tile in range(TILES):
            now = []
            for place in range(4):
                if place in (0, 3):
                    get = lambda c: halo[c, place // 3, tile]
                else:
                    get = lambda c: edge_coef[c, place - 1, tile]
                if k == 0 and place in (0, 3):
                    now.append([zero] * 3)
                else:
                    now.append(sums(get, [field[dc, place, tile] for dc in range(3)]))
            total = []
            for place in range(4):
                before = (None, now[0][2], saved[k, 1, tile], now[2][2])[place]
                after = (now[1][0], saved[k, 0, tile], now[3][0], None)[place]
                total.append(now[place][1] + north_of(before, now[place][2], row) + south_of(now[place][0], after, row))
            if k < 4:
                low, high = added[0, tile], added[1, tile]
                total[0] = total[0] + jnp.where(row == 7 - k, low, 0.0)
                total[3] = total[3] + jnp.where(row == k, high, 0.0)
                if k == 0:
                    total[1] = total[1] + jnp.where(row == 0, low, 0.0)
                    total[2] = total[2] + jnp.where(row == 7, high, 0.0)
                else:
                    total[0] = total[0] + jnp.where(row == 8 - k, turn(low, 4, 0), 0.0)
                    total[3] = total[3] + jnp.where(row == k - 1, turn(high, 4, 0), 0.0)
            for place in range(4):
                new[place].append(total[place])
        if k < STEPS - 1:
            for place in range(4):
                for dc in (-1, 0, 1):
                    for tile, x in enumerate(new[place] if dc == 0 else shifted(new[place], dc, lane)):
                        field[dc + 1, place, tile] = x
        else:
            for side in range(2):
                rows = slice(0, 8) if side == 0 else slice(SIZE - 8, SIZE)
                for level in range(LEVELS):
                    x = turn(new[1 + side][level], -(16 * level + 8))
                    out[level, rows, :] = edge_wet[side, level] * x


VMEM = pl.BlockSpec(memory_space=pltpu.VMEM)


def call(body, args, outs, scratch=(), flops=1000000, near=True, far_args=False):
    kind = pltpu.VMEM if near else jax.ShapeDtypeStruct
    return pl.pallas_call(
        body,
        out_shape=[kind(*(out if isinstance(out[0], tuple) else (out, F32))) for out in outs],
        in_specs=[pl.BlockSpec(memory_space=pl.ANY) if far_args else VMEM] * len(args),
        out_specs=[VMEM] * len(outs),
        scratch_shapes=[pltpu.VMEM(shape, F32) if isinstance(shape, tuple) else shape for shape in scratch],
        compiler_params=pltpu.CompilerParams(vmem_limit_bytes=40 * 1024 * 1024),
        cost_estimate=pl.CostEstimate(flops=flops, bytes_accessed=4 * 1024 * 1024, transcendentals=0),
        name=body.__name__,
    )(*args)


def shards(cotangent, coefficients, wet_mask):
    num_lon, num_lat = lax.axis_size("lon"), lax.axis_size("lat")

    def shift_lon(x, by):
        return lax.ppermute(x, "lon", [(i, (i + by) % num_lon) for i in range(num_lon)])

    def swap_chip(x):
        pairs = [[i, i + 1] for i in range(0, num_lat, 2)]
        return lax.all_gather(x, "lat", axis_index_groups=pairs)

    def swap_far(x):
        pairs = []
        for lon in range(num_lon):
            for lat in range(1, num_lat - 1):
                pairs.append((lon * num_lat + lat, lon * num_lat + ((lat + 1) ^ 1) - 1))
            pairs.append((lon * num_lat + num_lat - 1, (num_lon - 1 - lon) * num_lat + num_lat - 1))
        return lax.ppermute(x, ("lon", "lat"), pairs)

    fields = [pltpu.with_memory_space_constraint(x, pltpu.HBM) for x in (cotangent, coefficients, wet_mask)]
    whole = (LEVELS, SIZE, SIZE)
    lon1, lon2, masked, cot, wet = call(
        pack_lon,
        fields,
        [(288, SIZE), (288, SIZE), ((SIZE, 36 * SIZE), BF16), whole, (whole, jnp.int32)],
        [pltpu.VMEM((9,) + whole, BF16), pltpu.VMEM((2, 20 * SIZE, 2 * SIZE), BF16), pltpu.SemaphoreType.DMA((5,))],
        far_args=True,
    )
    got1 = shift_lon(lon1, 1)
    got2 = shift_lon(lon2, -1)
    main = call(rotate_main, (masked, cot, lon1), [(12,) + whole])[0]
    lat1, lat2 = call(pack_lat, (main, got1, got2), [(SENT, 8, SIZE)] * 2)
    far2 = swap_far(lat2)
    far1 = swap_chip(lat1)
    held = call(
        inner,
        (main, got1, got2, wet, lat2),
        [(9, 2, TILES, 8, SIZE), (3, 2, TILES, 8, SIZE), (STEPS, 2, TILES, 8, SIZE), whole, (2, LEVELS, 8, SIZE)],
        [(9, TILES, SIZE, SIZE), (3, TILES, SIZE, SIZE), (3, TILES, SIZE, SIZE)],
        flops=30000000,
    )
    return call(
        finish,
        tuple(held) + (far1, far2),
        [whole],
        [(3, 4, TILES, 8, SIZE), (9, 2, TILES, 8, SIZE), (2, TILES, 8, SIZE)],
        near=False,
    )[0]


def solution(mesh):
    in_specs = (P(None, "lat", "lon"), P(None, None, "lat", "lon"), P(None, "lat", "lon"))
    out_specs = P(None, "lat", "lon")
    return jax.shard_map(shards, mesh=mesh, in_specs=in_specs, out_specs=out_specs, check_vma=False)
```
